32 devices in a mesh: ctx: 8 (over y, x, core), ch: 4 (over z).
Axes of the slice: x: 2, y: 2, z: 4, core: 2. Of those that a mesh axis runs over, the one named last changes fastest.
Arguments:
- hidden: bfloat16 [8192, 8192], P('ch', 'ctx'), may hold values from -24 to 24
- cotangent: bfloat16 [8192, 8192], P('ch', 'ctx'), may hold values from -24 to 24
- norm_gain: float32 [8192], P('ch'), may hold values from 0.5 to 1.5
- mr_filter: bfloat16 [512, 128], P('ch'), may hold values from -0.5 to 0.5
- residue: float32 [512, 16], P('ch'), may hold values from -1.5 to 1.5
- decay_rate: float32 [512, 16], P('ch'), may hold values from 1.9073486e-06 to 0.033
- skip_weight: float32 [8192], P('ch'), may hold values from -3 to 3
Outputs:
- grad_hidden: bfloat16 [8192, 8192], P('ch', 'ctx')
- grad_gain: float32 [8192], P('ch')
- grad_mr: float32 [512, 128], P('ch')
- grad_residue: float32 [512, 16], P('ch')
- grad_log_rate: float32 [512, 16], P('ch')
- grad_skip: float32 [8192], P('ch')
- grad_inv_rms: float32 [8192], P('ctx')
The draws below stay inside these ranges and needn't reach their ends.
All inputs are finite; a program needn't handle non-finite values.
Results may differ from the reference program's by a relative error of at most 0.005.
Values may be sent and summed in bfloat16 or wider, within the bound.
A program may use at most 192 MiB of HBM per device.

```python
import math
import jax
import jax.numpy as jnp
from jax import lax

D = 8192
GROUP = 16
TAPS = 128
MODES = 16
GROUPS = 512
SEQ = 8192


def draw_hidden(key, part):
    first_key, second_key = jax.random.split(key, 2)
    values = jax.random.normal(first_key, (D, SEQ), jnp.float32)
    channel_pos = jnp.arange(D).astype(jnp.float32) / D
    roughness = jax.random.uniform(second_key, (D, 1), jnp.float32, 0.6, 1.4)
    scales = jnp.exp(jnp.log(3.0) * channel_pos)[:, None] * roughness
    return jnp.clip(values * scales, -24.0, 24.0).astype(jnp.bfloat16)


def draw_cotangent(key, part):
    first_key, second_key = jax.random.split(key, 2)
    values = jax.random.normal(first_key, (D, SEQ), jnp.float32)
    token_pos = jnp.arange(SEQ).astype(jnp.float32) / SEQ
    roughness = jax.random.uniform(second_key, (1, SEQ), jnp.float32, 0.6, 1.4)
    scales = jnp.exp(jnp.log(3.0) * token_pos)[None, :] * roughness
    return jnp.clip(values * scales, -24.0, 24.0).astype(jnp.bfloat16)


def steps_of(rng, shape, cuts, low, high):
    factor_of = 1.0
    for axis_at, shards_of in cuts:
        steps = jax.random.uniform(jax.random.fold_in(jax.random.fold_in(rng, 6), axis_at), (shards_of,), jnp.float32, low / len(cuts), high / len(cuts))
        factor_of = factor_of * jnp.repeat(jnp.exp(steps), shape[axis_at] // shards_of).reshape((-1,) + (1,) * (len(shape) - 1 - axis_at))
    return factor_of


def scatter_about(rng, dims, deviation, reach, cuts=(), kind=jnp.bfloat16):
    entries = jax.random.normal(rng, dims, jnp.float32) * deviation
    if len(cuts) > 0:
        entries = steps_of(rng, dims, cuts, -0.22, 0.18) * entries
    return jnp.clip(entries, min=-reach, max=reach).astype(kind)


def setup_inputs(seed: int = 0) -> dict:
    key_list = jax.random.split(jax.random.key(seed), 8)
    hidden = draw_hidden(jax.random.fold_in(key_list[7], 71), 0)
    cotangent = draw_cotangent(jax.random.fold_in(key_list[7], 71), 0)
    norm_gain = jnp.clip(1.0 + 0.1 * jax.random.normal(key_list[2], (D,), jnp.float32), 0.5, 1.5)
    mr_filter = scatter_about(key_list[3], (GROUPS, TAPS), TAPS ** -0.5, 0.5, ((0, 4),))
    residue = scatter_about(key_list[4], (GROUPS, MODES), 0.25, 1.5, ((0, 4),), jnp.float32)
    decay_rate = jnp.clip(jnp.exp(math.log(0.033) - 9.758549 * jax.random.uniform(key_list[5], (GROUPS, MODES), jnp.float32) ** steps_of(key_list[5], (GROUPS, MODES), ((0, 4),), -0.2, 0.2)), 1.9073486328125e-06, 0.033)
    skip_weight = scatter_about(key_list[6], (D,), 0.5, 3.0, ((0, 4),), jnp.float32)
    return dict(hidden=hidden, cotangent=cotangent, norm_gain=norm_gain, mr_filter=mr_filter, residue=residue, decay_rate=decay_rate, skip_weight=skip_weight)


eps_norm = 1e-06
top_precision = lax.Precision.HIGHEST

def reference(hidden, cotangent, norm_gain, mr_filter, residue, decay_rate, skip_weight):
    block_width = 16 * GROUP
    block_total = D // block_width
    group_count = block_width // GROUP
    grad_scale = SEQ ** (-0.5)
    fft_length = 2 * SEQ
    lag_values = jnp.arange(SEQ).astype(jnp.float32)

    def add_squares(running, block_index):
        hidden_rows = lax.dynamic_slice_in_dim(hidden, block_index * block_width, block_width, 0).astype(jnp.float32)
        return (running + lax.optimization_barrier(jnp.sum(hidden_rows * hidden_rows, axis=0)), None)
    squares, _ignored = lax.scan(add_squares, jnp.zeros((SEQ,), jnp.float32), jnp.arange(block_total))
    inverse_rms = lax.rsqrt(squares / D + eps_norm)

    def one_block(dot_running, block_index):
        start = block_index * block_width
        group_start = block_index * group_count
        hidden_rows = lax.dynamic_slice_in_dim(hidden, start, block_width, 0).astype(jnp.float32)
        grad_rows = lax.dynamic_slice_in_dim(cotangent, start, block_width, 0).astype(jnp.float32)
        gains = lax.dynamic_slice_in_dim(norm_gain, start, block_width, 0)
        skips = lax.dynamic_slice_in_dim(skip_weight, start, block_width, 0)
        short_taps = lax.dynamic_slice_in_dim(mr_filter, group_start, group_count, 0).astype(jnp.float32)
        residues = lax.dynamic_slice_in_dim(residue, group_start, group_count, 0)
        rates = lax.dynamic_slice_in_dim(decay_rate, group_start, group_count, 0)
        normed = hidden_rows * inverse_rms[None, :]
        normal_unit = lax.optimization_barrier((normed * gains[:, None]).astype(jnp.bfloat16)).astype(jnp.float32)
        channel_taps = jnp.repeat(short_taps, GROUP, axis=0)
        padded = jnp.pad(normal_unit, ((0, 0), (TAPS - 1, 0)))

        def forward_tap(tap_index, running):
            piece = lax.dynamic_slice_in_dim(padded, TAPS - 1 - tap_index, SEQ, 1)
            weight_col = lax.dynamic_slice_in_dim(channel_taps, tap_index, 1, 1)
            return running + weight_col * piece
        mixed = lax.fori_loop(0, TAPS, forward_tap, jnp.zeros((block_width, SEQ), jnp.float32))
        mixed = lax.optimization_barrier(mixed.astype(jnp.bfloat16)).astype(jnp.float32)
        amplitude = residues * jnp.sqrt(2.0 * rates)
        powers = jnp.exp(-rates[:, :, None] * lag_values[None, None, :])
        long_kernel = jnp.einsum('gn,gnt->gt', amplitude, powers, precision=top_precision)
        kernel_freq = jnp.repeat(jnp.fft.rfft(long_kernel, fft_length, axis=1), GROUP, axis=0)
        reversed_grad = jnp.fft.rfft(grad_rows[:, ::-1], fft_length, axis=1)
        correlated = jnp.fft.irfft(kernel_freq * reversed_grad, fft_length, axis=1)[:, :SEQ][:, ::-1]
        grad_mixed = lax.optimization_barrier((correlated + skips[:, None] * grad_rows).astype(jnp.bfloat16)).astype(jnp.float32)
        skip_grad = lax.optimization_barrier(jnp.sum(grad_rows * mixed, axis=1)) * grad_scale
        cross_freq = jnp.fft.rfft(grad_rows, fft_length, axis=1) * jnp.fft.rfft(mixed[:, ::-1], fft_length, axis=1)
        cross_freq = lax.optimization_barrier(jnp.sum(cross_freq.reshape(group_count, GROUP, -1), axis=1))
        lag_corr = jnp.fft.irfft(cross_freq, fft_length, axis=1)[:, SEQ - 1:2 * SEQ - 1]
        first_moment = jnp.einsum('gt,gnt->gn', lag_corr, powers, precision=top_precision)
        second_moment = jnp.einsum('gt,gnt->gn', lag_corr * lag_values[None, :], powers, precision=top_precision)
        residue_grad = jnp.sqrt(2.0 * rates) * first_moment * grad_scale
        rate_grad = amplitude * (0.5 * first_moment - rates * second_moment) * grad_scale
        grad_padded = jnp.pad(grad_mixed, ((0, 0), (0, TAPS - 1)))

        def backward_tap(tap_index, carried):
            running, tap_terms = carried
            ahead = lax.dynamic_slice_in_dim(grad_padded, tap_index, SEQ, 1)
            weight_col = lax.dynamic_slice_in_dim(channel_taps, tap_index, 1, 1)
            behind = lax.dynamic_slice_in_dim(padded, TAPS - 1 - tap_index, SEQ, 1)
            term = lax.optimization_barrier(jnp.sum(grad_mixed * behind, axis=1))
            tap_terms = lax.dynamic_update_slice_in_dim(tap_terms, term[:, None], tap_index, 1)
            return (running + weight_col * ahead, tap_terms)
        input_grad, tap_terms = lax.fori_loop(0, TAPS, backward_tap, (jnp.zeros((block_width, SEQ), jnp.float32), jnp.zeros((block_width, TAPS), jnp.float32)))
        short_grad = lax.optimization_barrier(jnp.sum(tap_terms.reshape(group_count, GROUP, TAPS), axis=1)) * grad_scale
        pulled = input_grad * gains[:, None]
        gain_grad = lax.optimization_barrier(jnp.sum(input_grad * normed, axis=1)) * grad_scale
        dot_running = dot_running + lax.optimization_barrier(jnp.sum(pulled * normed, axis=0))
        return (dot_running, (pulled, gain_grad, short_grad, residue_grad, rate_grad, skip_grad))
    row_dot, results = lax.scan(one_block, jnp.zeros((SEQ,), jnp.float32), jnp.arange(block_total))
    pulled_all, gain_all, short_all, residue_all, rate_all, skip_all = results
    grad_inv_rms = row_dot / inverse_rms * D ** (-0.5)

    def finish_block(pieces):
        block_index, pulled = pieces
        hidden_rows = lax.dynamic_slice_in_dim(hidden, block_index * block_width, block_width, 0).astype(jnp.float32)
        normed = hidden_rows * inverse_rms[None, :]
        return (inverse_rms[None, :] * (pulled - normed * row_dot[None, :] / D)).astype(jnp.bfloat16)
    grad_hidden = lax.map(finish_block, (jnp.arange(block_total), pulled_all)).reshape(D, SEQ)
    return (grad_hidden, gain_all.reshape(D), short_all.reshape(GROUPS, TAPS), residue_all.reshape(GROUPS, MODES), rate_all.reshape(GROUPS, MODES), skip_all.reshape(D), grad_inv_rms)
```

```python
import functools

import jax
import jax.numpy as jnp
from jax import lax
from jax.experimental import pallas as pl
from jax.experimental.pallas import tpu as pltpu
from jax.sharding import PartitionSpec as P

eps_norm = 1e-06
W = 128
GW = 16
PACK = W // GW
VMEM_LIMIT = 48 * 1024 * 1024


def passed_along(x, axis, by):
    count = lax.axis_size(axis)
    pairs = [(i, i + by) for i in range(count) if 0 <= i + by < count]
    return lax.ppermute(x, axis, pairs)


def dot(a, b, ca, cb):
    return lax.dot_general(
        a, b, (((ca,), (cb,)), ((), ())), preferred_element_type=jnp.float32
    )


def columns_of(row):
    return jnp.broadcast_to(row, (W, W)).T


def row_sums(stack):
    return jnp.sum(stack.T, axis=0, keepdims=True)


def split_two(x):
    high = x.astype(jnp.bfloat16)
    return high, (x - high.astype(jnp.float32)).astype(jnp.bfloat16)


def circulant(row):
    return pltpu.roll(jnp.broadcast_to(row, (W, W)), 0, 1, stride=1, stride_axis=0)


def diagonal_sums(x):
    half = W // 2
    while half >= 8:
        x = x[:half] + pltpu.roll(x[half:], W - half, 1)
        half //= 2
    for by in (4, 2, 1):
        x = x + pltpu.roll(pltpu.roll(x, W - by, 1), 8 - by, 0)
    return x[:1]


def tiles_of(ref, rows, blocks):
    return [ref[rows, W * k : W * (k + 1)] for k in range(blocks)]


def state_kernel(rate_ref, g_ref, ga_ref, s0_ref, s1_ref, total_ref):
    blocks = g_ref.shape[1] // W
    rates = columns_of(rate_ref[0])
    lane_int = lax.broadcasted_iota(jnp.int32, (GW, W), 1)
    lane = lane_int.astype(jnp.float32)
    seg = lane_int // GW
    total0 = jnp.zeros((GW, W), jnp.float32)
    total1 = jnp.zeros((GW, W), jnp.float32)
    for q in range(PACK):
        rows = slice(GW * q, GW * (q + 1))
        r = rates[rows]
        fall = jnp.exp(-r * lane)
        table = jnp.concatenate(split_two(fall) + split_two(fall * lane), axis=0)
        data = jnp.concatenate(tiles_of(g_ref, rows, blocks)[1:] + [ga_ref[rows, :]], axis=0)
        sums = dot(table, data, 1, 1)
        s0 = sums[:GW] + sums[GW : 2 * GW]
        s1 = sums[2 * GW : 3 * GW] + sums[3 * GW :]
        by = 1
        while by < blocks:
            decay = jnp.exp(-r * float(W * by))
            keep = seg + by < blocks
            a0 = jnp.where(keep, pltpu.roll(s0, W - GW * by, 1), 0.0)
            a1 = jnp.where(keep, pltpu.roll(s1, W - GW * by, 1), 0.0)
            s1 = s1 + decay * (a1 + float(W * by) * a0)
            s0 = s0 + decay * a0
            by *= 2
        s0_ref[q] = s0
        s1_ref[q] = s1
        here = seg == q
        total0 = jnp.where(here, pltpu.roll(s0, GW * q, 1) if q else s0, total0)
        total1 = jnp.where(here, pltpu.roll(s1, GW * q, 1) if q else s1, total1)
    total_ref[0, :GW] = total0
    total_ref[0, GW:] = total1


def main_kernel(
    rank_ref, rate_ref, res_ref, gain_ref, skip_ref, tap_ref, inv_ref, h_ref, hb_ref, g_ref, ga_ref,
    s0_ref, s1_ref, total_ref,
    ig_ref, tapg_ref, mom0_ref, mom1_ref, skipg_ref, gaing_ref, dot_ref,
):
    tokens = g_ref.shape[1]
    blocks = tokens // W
    count = total_ref.shape[0]
    rank = rank_ref[0]
    rates = columns_of(rate_ref[0])
    residues = columns_of(res_ref[0])
    gains = columns_of(gain_ref[0])
    skips = columns_of(skip_ref[0])
    lane_int = lax.broadcasted_iota(jnp.int32, (GW, W), 1)
    lane = lane_int.astype(jnp.float32)
    seg = lane_int // GW
    upper = lax.broadcasted_iota(jnp.int32, (W, W), 1) >= lax.broadcasted_iota(
        jnp.int32, (W, W), 0
    )
    rate_seg = jnp.zeros((GW, W), jnp.float32)
    for q in range(PACK):
        rate_seg = jnp.where(seg == q, rates[GW * q : GW * (q + 1)], rate_seg)
    in0 = jnp.zeros((GW, W), jnp.float32)
    in1 = jnp.zeros((GW, W), jnp.float32)
    for m in range(1, count):
        gap = m - rank - 1
        span = (jnp.maximum(gap, 0) * tokens).astype(jnp.float32)
        factor = jnp.where(gap >= 0, jnp.exp(-rate_seg * span), 0.0)
        t0 = total_ref[m, 0, :GW]
        in0 = in0 + factor * t0
        in1 = in1 + factor * (total_ref[m, 0, GW:] + span * t0)
    left = ((blocks - seg) * W).astype(jnp.float32)

    @pl.when(pl.program_id(0) == 0)
    def _():
        dot_ref[...] = jnp.zeros_like(dot_ref)

    inv_back = inv_ref[:, :W]
    inv = [inv_ref[:, W * (k + 1) : W * (k + 2)] for k in range(blocks)]
    moments0, moments1, skip_rows, gain_rows = [], [], [], []
    dots = None
    for q in range(PACK):
        rows = slice(GW * q, GW * (q + 1))
        r = rates[rows]
        amp = residues[rows] * jnp.sqrt(2.0 * r)
        gain = gains[rows]
        skip = skips[rows]
        fall = jnp.exp(-r * lane)
        kern = jnp.sum(amp * fall, axis=0, keepdims=True)
        kern_high, kern_low = split_two(jnp.where(upper, circulant(kern), 0.0))
        circ = circulant(tap_ref[q : q + 1, :])
        now = jnp.where(upper, circ, 0.0).astype(jnp.bfloat16)
        before = jnp.where(upper, 0.0, circ).astype(jnp.bfloat16)
        normed = [t.astype(jnp.float32) * i for t, i in zip(tiles_of(h_ref, rows, blocks), inv)]
        units = [(n * gain).astype(jnp.bfloat16) for n in normed]
        unit_back = (hb_ref[rows, :].astype(jnp.float32) * inv_back * gain).astype(jnp.bfloat16)
        x_now = jnp.concatenate(units, axis=0)
        x_before = jnp.concatenate([unit_back] + units[:-1], axis=0)
        mixed = (dot(x_now, now, 1, 0) + dot(x_before, before, 1, 0)).astype(jnp.bfloat16)
        g_tiles = tiles_of(g_ref, rows, blocks)
        grads = jnp.concatenate(g_tiles, axis=0)
        grads_long = jnp.concatenate(g_tiles + [ga_ref[rows, :]], axis=0)
        a0in = jnp.where(seg == q, in0, 0.0)
        a1in = jnp.where(seg == q, in1, 0.0)
        for by in (GW, 2 * GW, 4 * GW):
            a0in = a0in + pltpu.roll(a0in, by, 1)
            a1in = a1in + pltpu.roll(a1in, by, 1)
        decay = jnp.exp(-r * left)
        after0 = s0_ref[q] + decay * a0in
        after1 = s1_ref[q] + decay * (a1in + left * a0in)
        gap = float(W) - lane
        to_end = jnp.exp(-r * gap)
        a_high, a_low = split_two(jnp.concatenate([after0, a0in], axis=1))
        w_high, w_low = split_two(amp * to_end)
        outer = dot(
            jnp.concatenate([a_high, a_low, a_high], axis=0),
            jnp.concatenate([w_high, w_high, w_low], axis=0),
            0, 0,
        )[: W + GW]
        wide = grads_long.astype(jnp.float32)
        gm = (
            dot(grads_long, kern_high, 1, 1)
            + dot(grads_long, kern_low, 1, 1)
            + outer
            + jnp.concatenate([skip] * (blocks + 1), axis=0) * wide
        ).astype(jnp.bfloat16)
        gm_now = gm[:W]
        ig = dot(gm_now, now, 1, 1) + dot(gm[GW:], before, 1, 1)
        pairs = jnp.where(upper, dot(x_now, gm_now, 0, 0), dot(x_before, gm_now, 0, 0))
        tapg_ref[q : q + 1, :] = diagonal_sums(pairs)
        lags = diagonal_sums(jnp.where(upper, dot(mixed, grads, 0, 0), 0.0))
        table = jnp.concatenate(split_two(to_end) + split_two(to_end * gap), axis=0)
        lifted = dot(table, mixed, 1, 1)
        l0 = lifted[:GW] + lifted[GW : 2 * GW]
        l1 = lifted[2 * GW : 3 * GW] + lifted[3 * GW :]
        near = lags * fall
        moments0.append(l0 * after0 + near)
        moments1.append(l1 * after0 + l0 * after1 + near * lane)
        skip_terms = wide[:W] * mixed.astype(jnp.float32)
        gain_terms = ig * jnp.concatenate(normed, axis=0)
        skip_sum = skip_terms[:GW]
        gain_sum = gain_terms[:GW]
        for k in range(blocks):
            part = slice(GW * k, GW * (k + 1))
            ig_ref[rows, W * k : W * (k + 1)] = ig[part]
            if k:
                skip_sum = skip_sum + skip_terms[part]
                gain_sum = gain_sum + gain_terms[part]
        skip_rows.append(skip_sum)
        gain_rows.append(gain_sum)
        dot_ref[...] += gain_terms * jnp.concatenate([gain] * blocks, axis=0)
    mom0_ref[0] = row_sums(jnp.concatenate(moments0, axis=0))
    mom1_ref[0] = row_sums(jnp.concatenate(moments1, axis=0))
    skipg_ref[0] = row_sums(jnp.concatenate(skip_rows, axis=0))
    gaing_ref[0] = row_sums(jnp.concatenate(gain_rows, axis=0))


def local(hidden, cotangent, norm_gain, mr_filter, residue, decay_rate, skip_weight):
    channels, tokens = hidden.shape
    groups = mr_filter.shape[0]
    ctx_count = lax.axis_size("ctx")
    full_width = channels * lax.axis_size("ch")
    grad_scale = (tokens * ctx_count) ** (-0.5)
    steps = groups // PACK
    f32 = jnp.float32

    hidden_back = passed_along(hidden[:, tokens - W :], "ctx", 1)
    cot_ahead = passed_along(cotangent[:, :W], "ctx", -1)

    def squares_of(x):
        wide = x.astype(f32)
        return jnp.sum(wide * wide, axis=0)

    squares = lax.psum(
        jnp.concatenate([squares_of(hidden_back), squares_of(hidden)]), "ch"
    )
    inverse_all = lax.rsqrt(squares / full_width + eps_norm)
    inverse_rms = inverse_all[W:]

    rate_rows = decay_rate.reshape(steps, 1, W)
    residue_rows = residue.reshape(steps, 1, W)
    gain_rows = norm_gain.reshape(steps, 1, W)
    skip_rows = skip_weight.reshape(steps, 1, W)

    row_spec = pl.BlockSpec((1, 1, W), lambda i: (i, 0, 0))
    wide_spec = pl.BlockSpec((W, tokens), lambda i: (i, 0))
    edge_spec = pl.BlockSpec((W, W), lambda i: (i, 0))
    state_spec = pl.BlockSpec((PACK, GW, W), lambda i: (i, 0, 0))
    row_shape = jax.ShapeDtypeStruct((steps, 1, W), f32)
    state_shape = jax.ShapeDtypeStruct((groups, GW, W), f32)

    state0, state1, total = pl.pallas_call(
        state_kernel,
        grid=(steps,),
        in_specs=[row_spec, wide_spec, edge_spec],
        out_specs=[state_spec, state_spec, pl.BlockSpec((1, 2 * GW, W), lambda i: (i, 0, 0))],
        out_shape=[state_shape, state_shape, jax.ShapeDtypeStruct((steps, 2 * GW, W), f32)],
        compiler_params=pltpu.CompilerParams(vmem_limit_bytes=VMEM_LIMIT),
        cost_estimate=pl.CostEstimate(
            flops=groups * 2 * 64 * W * W, bytes_accessed=8 * 2**20, transcendentals=0
        ),
        name="states",
    )(rate_rows, cotangent, cot_ahead)
    totals = lax.all_gather(total, "ctx", axis=0, tiled=False)

    rank = lax.axis_index("ctx").astype(jnp.int32).reshape(1)
    input_grad, tap_part, mom0, mom1, skip_part, gain_part, dots = pl.pallas_call(
        main_kernel,
        grid=(steps,),
        in_specs=[
            pl.BlockSpec(memory_space=pltpu.SMEM),
            row_spec, row_spec, row_spec, row_spec,
            pl.BlockSpec((PACK, W), lambda i: (i, 0)),
            pl.BlockSpec((1, tokens + W), lambda i: (0, 0)),
            wide_spec, edge_spec, wide_spec, edge_spec,
            state_spec, state_spec,
            pl.BlockSpec((ctx_count, 1, 2 * GW, W), lambda i: (0, i, 0, 0)),
        ],
        out_specs=[
            wide_spec,
            pl.BlockSpec((PACK, W), lambda i: (i, 0)),
            row_spec, row_spec, row_spec, row_spec,
            pl.BlockSpec((W, W), lambda i: (0, 0)),
        ],
        out_shape=[
            jax.ShapeDtypeStruct((channels, tokens), f32),
            jax.ShapeDtypeStruct((groups, W), f32),
            row_shape, row_shape, row_shape, row_shape,
            jax.ShapeDtypeStruct((W, W), f32),
        ],
        compiler_params=pltpu.CompilerParams(vmem_limit_bytes=VMEM_LIMIT),
        cost_estimate=pl.CostEstimate(
            flops=groups * 24 * W**3, bytes_accessed=24 * 2**20, transcendentals=0
        ),
        name="main",
    )(
        rank, rate_rows, residue_rows, gain_rows, skip_rows, mr_filter.astype(f32),
        inverse_all.reshape(1, tokens + W), hidden, hidden_back, cotangent, cot_ahead,
        state0, state1, totals,
    )
    row_dot = lax.psum(
        jnp.sum(dots.reshape(tokens // W, GW, W), axis=1).reshape(tokens), "ch"
    )
    parts = jnp.concatenate(
        [tap_part] + [x.reshape(steps, W) for x in (mom0, mom1, skip_part, gain_part)], axis=0
    )
    whole = jnp.sum(lax.all_gather(parts, "ctx", axis=0, tiled=False), axis=0)
    tap_total = whole[:groups]
    first, second, skip_total, gain_total = (
        whole[groups + steps * i : groups + steps * (i + 1)] for i in range(4)
    )
    first_moment = first.reshape(decay_rate.shape)
    second_moment = second.reshape(decay_rate.shape)

    normed = hidden.astype(f32) * inverse_rms[None, :]
    pulled = input_grad * norm_gain[:, None]
    grad_inv_rms = row_dot / inverse_rms * full_width ** (-0.5)
    grad_hidden = (inverse_rms[None, :] * (pulled - normed * row_dot[None, :] / full_width)).astype(
        jnp.bfloat16
    )
    root_rate = jnp.sqrt(2.0 * decay_rate)
    grad_residue = root_rate * first_moment * grad_scale
    grad_log_rate = (
        residue * root_rate * (0.5 * first_moment - decay_rate * second_moment) * grad_scale
    )
    return (
        grad_hidden,
        gain_total.reshape(channels) * grad_scale,
        tap_total * grad_scale,
        grad_residue,
        grad_log_rate,
        skip_total.reshape(channels) * grad_scale,
        grad_inv_rms,
    )


def solution(mesh):
    return jax.shard_map(
        local,
        mesh=mesh,
        in_specs=(
            P("ch", "ctx"),
            P("ch", "ctx"),
            P("ch"),
            P("ch", None),
            P("ch", None),
            P("ch", None),
            P("ch"),
        ),
        out_specs=(
            P("ch", "ctx"),
            P("ch"),
            P("ch", None),
            P("ch", None),
            P("ch", None),
            P("ch"),
            P("ctx"),
        ),
        check_vma=False,
    )
```

```python
import functools

import jax
import jax.numpy as jnp
from jax import lax
from jax.experimental import pallas as pl
from jax.experimental.pallas import tpu as pltpu
from jax.sharding import PartitionSpec as P

eps_norm = 1e-06
W = 128
GW = 16
PACK = W // GW
VMEM_LIMIT = 48 * 1024 * 1024


def passed_along(x, axis, by):
    count = lax.axis_size(axis)
    pairs = [(i, i + by) for i in range(count) if 0 <= i + by < count]
    return lax.ppermute(x, axis, pairs)


def exchanged(x, axis, bit):
    count = lax.axis_size(axis)
    return lax.ppermute(x, axis, [(i, i ^ bit) for i in range(count)])


def sum_over(x, axis):
    bit = 1
    while bit < lax.axis_size(axis):
        x = x + exchanged(x, axis, bit)
        bit *= 2
    return x


def states_after(total, rates, tokens):
    count = lax.axis_size("ctx")
    rank = lax.axis_index("ctx")
    into0 = jnp.zeros_like(rates)
    into1 = jnp.zeros_like(rates)
    bit = 1
    while bit < count:
        other = exchanged(total, "ctx", bit)
        o0, o1 = other[:, :GW], other[:, GW:]
        t0, t1 = total[:, :GW], total[:, GW:]
        lower = (rank & bit) == 0
        start = (rank // bit + 1) * bit
        gap = ((start - rank - 1) * tokens).astype(jnp.float32)
        factor = jnp.where(lower, jnp.exp(-rates * gap), 0.0)
        into0 = into0 + factor * o0
        into1 = into1 + factor * (o1 + gap * o0)
        if 2 * bit < count:
            span = float(bit * tokens)
            decay = jnp.exp(-rates * span)
            e0, e1 = jnp.where(lower, t0, o0), jnp.where(lower, t1, o1)
            l0, l1 = jnp.where(lower, o0, t0), jnp.where(lower, o1, t1)
            total = jnp.concatenate([e0 + decay * l0, e1 + decay * (l1 + span * l0)], axis=1)
        bit *= 2
    return jnp.concatenate([into0, into1], axis=1)


def dot(a, b, ca, cb):
    return lax.dot_general(
        a, b, (((ca,), (cb,)), ((), ())), preferred_element_type=jnp.float32
    )


def columns_of(row):
    return jnp.broadcast_to(row, (W, W)).T


def row_sums(stack):
    return jnp.sum(stack.T, axis=0, keepdims=True)


def split_two(x):
    high = x.astype(jnp.bfloat16)
    return high, (x - high.astype(jnp.float32)).astype(jnp.bfloat16)


def circulant(row):
    return pltpu.roll(jnp.broadcast_to(row, (W, W)), 0, 1, stride=1, stride_axis=0)


def diagonal_sums(x):
    half = W // 2
    while half >= 8:
        x = x[:half] + pltpu.roll(x[half:], W - half, 1)
        half //= 2
    for by in (4, 2, 1):
        x = x + pltpu.roll(pltpu.roll(x, W - by, 1), 8 - by, 0)
    return x[:1]


def tiles_of(ref, rows, blocks):
    return [ref[rows, W * k : W * (k + 1)] for k in range(blocks)]


def state_kernel(rate_ref, g_ref, ga_ref, s0_ref, s1_ref, total_ref, seg_rate_ref):
    blocks = g_ref.shape[1] // W
    rates = columns_of(rate_ref[0])
    lane_int = lax.broadcasted_iota(jnp.int32, (GW, W), 1)
    lane = lane_int.astype(jnp.float32)
    seg = lane_int // GW
    rate_seg = jnp.zeros((GW, W), jnp.float32)
    total0 = jnp.zeros((GW, W), jnp.float32)
    total1 = jnp.zeros((GW, W), jnp.float32)
    for q in range(PACK):
        rows = slice(GW * q, GW * (q + 1))
        r = rates[rows]
        fall = jnp.exp(-r * lane)
        table = jnp.concatenate(split_two(fall) + split_two(fall * lane), axis=0)
        data = jnp.concatenate(tiles_of(g_ref, rows, blocks)[1:] + [ga_ref[rows, :]], axis=0)
        sums = dot(table, data, 1, 1)
        s0 = sums[:GW] + sums[GW : 2 * GW]
        s1 = sums[2 * GW : 3 * GW] + sums[3 * GW :]
        by = 1
        while by < blocks:
            decay = jnp.exp(-r * float(W * by))
            keep = seg + by < blocks
            a0 = jnp.where(keep, pltpu.roll(s0, W - GW * by, 1), 0.0)
            a1 = jnp.where(keep, pltpu.roll(s1, W - GW * by, 1), 0.0)
            s1 = s1 + decay * (a1 + float(W * by) * a0)
            s0 = s0 + decay * a0
            by *= 2
        s0_ref[q] = s0
        s1_ref[q] = s1
        here = seg == q
        rate_seg = jnp.where(here, r, rate_seg)
        total0 = jnp.where(here, pltpu.roll(s0, GW * q, 1) if q else s0, total0)
        total1 = jnp.where(here, pltpu.roll(s1, GW * q, 1) if q else s1, total1)
    total_ref[0, :GW] = total0
    total_ref[0, GW:] = total1
    seg_rate_ref[0] = rate_seg


def main_kernel(
    rate_ref, res_ref, gain_ref, skip_ref, tap_ref, inv_ref, h_ref, hb_ref, g_ref, ga_ref,
    s0_ref, s1_ref, into_ref,
    ig_ref, tapg_ref, mom0_ref, mom1_ref, skipg_ref, gaing_ref, dot_ref,
):
    tokens = g_ref.shape[1]
    blocks = tokens // W
    rates = columns_of(rate_ref[0])
    residues = columns_of(res_ref[0])
    gains = columns_of(gain_ref[0])
    skips = columns_of(skip_ref[0])
    lane_int = lax.broadcasted_iota(jnp.int32, (GW, W), 1)
    lane = lane_int.astype(jnp.float32)
    seg = lane_int // GW
    upper = lax.broadcasted_iota(jnp.int32, (W, W), 1) >= lax.broadcasted_iota(
        jnp.int32, (W, W), 0
    )
    lower = lax.broadcasted_iota(jnp.int32, (W, W), 1) <= lax.broadcasted_iota(
        jnp.int32, (W, W), 0
    )
    back = jnp.where(lane_int == 0, 0.0, float(W) - lane)
    gap = float(W) - lane
    in0 = into_ref[0, :GW]
    in1 = into_ref[0, GW:]
    left = ((blocks - seg) * W).astype(jnp.float32)

    @pl.when(pl.program_id(0) == 0)
    def _():
        dot_ref[...] = jnp.zeros_like(dot_ref)

    inv_back = inv_ref[:, :W]
    inv = [inv_ref[:, W * (k + 1) : W * (k + 2)] for k in range(blocks)]
    moments0, moments1, skip_rows, gain_rows = [], [], [], []
    dots = None
    for q in range(PACK):
        rows = slice(GW * q, GW * (q + 1))
        r = rates[rows]
        amp = residues[rows] * jnp.sqrt(2.0 * r)
        gain = gains[rows]
        skip = skips[rows]
        to_end = jnp.exp(-r * gap)
        fall = jnp.where(lane_int == 0, 1.0, to_end)
        kern = jnp.sum(amp * fall, axis=0, keepdims=True)
        kern_two = jnp.concatenate(
            split_two(jnp.where(lower, circulant(kern), 0.0)), axis=0
        )
        circ = circulant(tap_ref[q : q + 1, :])
        now = jnp.where(upper, circ, 0.0).astype(jnp.bfloat16)
        before = jnp.where(upper, 0.0, circ).astype(jnp.bfloat16)
        normed = [t.astype(jnp.float32) * i for t, i in zip(tiles_of(h_ref, rows, blocks), inv)]
        units = [(n * gain).astype(jnp.bfloat16) for n in normed]
        unit_back = (hb_ref[rows, :].astype(jnp.float32) * inv_back * gain).astype(jnp.bfloat16)
        x_now = jnp.concatenate(units, axis=0)
        x_before = jnp.concatenate([unit_back] + units[:-1], axis=0)
        x_both = jnp.concatenate([x_now, x_before], axis=1)
        mixed = dot(x_both, jnp.concatenate([now, before], axis=0), 1, 0).astype(jnp.bfloat16)
        g_tiles = tiles_of(g_ref, rows, blocks)
        grads = jnp.concatenate(g_tiles, axis=0)
        grads_long = jnp.concatenate(g_tiles + [ga_ref[rows, :]], axis=0)
        a0in = jnp.where(seg == q, in0, 0.0)
        a1in = jnp.where(seg == q, in1, 0.0)
        for by in (GW, 2 * GW, 4 * GW):
            a0in = a0in + pltpu.roll(a0in, by, 1)
            a1in = a1in + pltpu.roll(a1in, by, 1)
        decay = jnp.exp(-r * left)
        after0 = s0_ref[q] + decay * a0in
        after1 = s1_ref[q] + decay * (a1in + left * a0in)
        a_high, a_low = split_two(jnp.concatenate([after0, a0in], axis=1))
        w_high, w_low = split_two(amp * to_end)
        outer = dot(
            jnp.concatenate([a_high, a_low, a_high], axis=0),
            jnp.concatenate([w_high, w_high, w_low], axis=0),
            0, 0,
        )[: W + GW]
        wide = grads_long.astype(jnp.float32)
        gm = (
            dot(jnp.concatenate([grads_long, grads_long], axis=1), kern_two, 1, 0)
            + outer
            + jnp.concatenate([skip] * (blocks + 1), axis=0) * wide
        ).astype(jnp.bfloat16)
        gm_now = gm[:W]
        ig = dot(
            jnp.concatenate([gm_now, gm[GW:]], axis=1),
            jnp.concatenate([now, before], axis=1),
            1, 1,
        )
        pairs = dot(gm_now, x_both, 0, 0)
        tapg_ref[q : q + 1, :] = diagonal_sums(jnp.where(lower, pairs[:, :W], pairs[:, W:]))
        lags = diagonal_sums(jnp.where(lower, dot(grads, mixed, 0, 0), 0.0))
        table = jnp.concatenate(split_two(to_end) + split_two(to_end * gap), axis=0)
        lifted = dot(table, mixed, 1, 1)
        l0 = lifted[:GW] + lifted[GW : 2 * GW]
        l1 = lifted[2 * GW : 3 * GW] + lifted[3 * GW :]
        near = lags * fall
        moments0.append(l0 * after0 + near)
        moments1.append(l1 * after0 + l0 * after1 + near * back)
        skip_terms = wide[:W] * mixed.astype(jnp.float32)
        gain_terms = ig * jnp.concatenate(normed, axis=0)
        skip_sum = skip_terms[:GW]
        gain_sum = gain_terms[:GW]
        for k in range(blocks):
            part = slice(GW * k, GW * (k + 1))
            ig_ref[rows, W * k : W * (k + 1)] = ig[part]
            if k:
                skip_sum = skip_sum + skip_terms[part]
                gain_sum = gain_sum + gain_terms[part]
        skip_rows.append(skip_sum)
        gain_rows.append(gain_sum)
        dot_ref[...] += gain_terms * jnp.concatenate([gain] * blocks, axis=0)
    mom0_ref[0] = row_sums(jnp.concatenate(moments0, axis=0))
    mom1_ref[0] = row_sums(jnp.concatenate(moments1, axis=0))
    skipg_ref[0] = row_sums(jnp.concatenate(skip_rows, axis=0))
    gaing_ref[0] = row_sums(jnp.concatenate(gain_rows, axis=0))


def local(hidden, cotangent, norm_gain, mr_filter, residue, decay_rate, skip_weight):
    channels, tokens = hidden.shape
    groups = mr_filter.shape[0]
    ctx_count = lax.axis_size("ctx")
    full_width = channels * lax.axis_size("ch")
    grad_scale = (tokens * ctx_count) ** (-0.5)
    steps = groups // PACK
    f32 = jnp.float32

    hidden_back = passed_along(hidden[:, tokens - W :], "ctx", 1)
    cot_ahead = passed_along(cotangent[:, :W], "ctx", -1)

    def squares_of(x):
        wide = x.astype(f32)
        return jnp.sum(wide * wide, axis=0)

    squares = sum_over(jnp.concatenate([squares_of(hidden_back), squares_of(hidden)]), "ch")
    inverse_all = lax.rsqrt(squares / full_width + eps_norm)
    inverse_rms = inverse_all[W:]

    rate_rows = decay_rate.reshape(steps, 1, W)
    residue_rows = residue.reshape(steps, 1, W)
    gain_rows = norm_gain.reshape(steps, 1, W)
    skip_rows = skip_weight.reshape(steps, 1, W)

    row_spec = pl.BlockSpec((1, 1, W), lambda i: (i, 0, 0))
    wide_spec = pl.BlockSpec((W, tokens), lambda i: (i, 0))
    edge_spec = pl.BlockSpec((W, W), lambda i: (i, 0))
    state_spec = pl.BlockSpec((PACK, GW, W), lambda i: (i, 0, 0))
    row_shape = jax.ShapeDtypeStruct((steps, 1, W), f32)
    state_shape = jax.ShapeDtypeStruct((groups, GW, W), f32)

    state0, state1, total, seg_rates = pl.pallas_call(
        state_kernel,
        grid=(steps,),
        in_specs=[row_spec, wide_spec, edge_spec],
        out_specs=[
            state_spec, state_spec,
            pl.BlockSpec((1, 2 * GW, W), lambda i: (i, 0, 0)),
            pl.BlockSpec((1, GW, W), lambda i: (i, 0, 0)),
        ],
        out_shape=[
            state_shape, state_shape,
            jax.ShapeDtypeStruct((steps, 2 * GW, W), f32),
            jax.ShapeDtypeStruct((steps, GW, W), f32),
        ],
        compiler_params=pltpu.CompilerParams(vmem_limit_bytes=VMEM_LIMIT),
        cost_estimate=pl.CostEstimate(
            flops=groups * 2 * 64 * W * W, bytes_accessed=8 * 2**20, transcendentals=0
        ),
        name="states",
    )(rate_rows, cotangent, cot_ahead)
    into = states_after(total, seg_rates, tokens)

    input_grad, tap_part, mom0, mom1, skip_part, gain_part, dots = pl.pallas_call(
        main_kernel,
        grid=(steps,),
        in_specs=[
            row_spec, row_spec, row_spec, row_spec,
            pl.BlockSpec((PACK, W), lambda i: (i, 0)),
            pl.BlockSpec((1, tokens + W), lambda i: (0, 0)),
            wide_spec, edge_spec, wide_spec, edge_spec,
            state_spec, state_spec,
            pl.BlockSpec((1, 2 * GW, W), lambda i: (i, 0, 0)),
        ],
        out_specs=[
            wide_spec,
            pl.BlockSpec((PACK, W), lambda i: (i, 0)),
            row_spec, row_spec, row_spec, row_spec,
            pl.BlockSpec((W, W), lambda i: (0, 0)),
        ],
        out_shape=[
            jax.ShapeDtypeStruct((channels, tokens), f32),
            jax.ShapeDtypeStruct((groups, W), f32),
            row_shape, row_shape, row_shape, row_shape,
            jax.ShapeDtypeStruct((W, W), f32),
        ],
        compiler_params=pltpu.CompilerParams(vmem_limit_bytes=VMEM_LIMIT),
        cost_estimate=pl.CostEstimate(
            flops=groups * 24 * W**3, bytes_accessed=24 * 2**20, transcendentals=0
        ),
        name="main",
    )(
        rate_rows, residue_rows, gain_rows, skip_rows, mr_filter.astype(f32),
        inverse_all.reshape(1, tokens + W), hidden, hidden_back, cotangent, cot_ahead,
        state0, state1, into,
    )
    row_dot = sum_over(jnp.sum(dots.reshape(tokens // W, GW, W), axis=1).reshape(tokens), "ch")
    parts = jnp.concatenate(
        [tap_part] + [x.reshape(steps, W) for x in (mom0, mom1, skip_part, gain_part)], axis=0
    )
    whole = sum_over(parts, "ctx")
    tap_total = jnp.roll(whole[:groups, ::-1], 1, axis=1)
    first, second, skip_total, gain_total = (
        whole[groups + steps * i : groups + steps * (i + 1)] for i in range(4)
    )
    first_moment = first.reshape(decay_rate.shape)
    second_moment = second.reshape(decay_rate.shape)

    normed = hidden.astype(f32) * inverse_rms[None, :]
    pulled = input_grad * norm_gain[:, None]
    grad_inv_rms = row_dot / inverse_rms * full_width ** (-0.5)
    grad_hidden = (inverse_rms[None, :] * (pulled - normed * row_dot[None, :] / full_width)).astype(
        jnp.bfloat16
    )
    root_rate = jnp.sqrt(2.0 * decay_rate)
    grad_residue = root_rate * first_moment * grad_scale
    grad_log_rate = (
        residue * root_rate * (0.5 * first_moment - decay_rate * second_moment) * grad_scale
    )
    return (
        grad_hidden,
        gain_total.reshape(channels) * grad_scale,
        tap_total * grad_scale,
        grad_residue,
        grad_log_rate,
        skip_total.reshape(channels) * grad_scale,
        grad_inv_rms,
    )


def solution(mesh):
    return jax.shard_map(
        local,
        mesh=mesh,
        in_specs=(
            P("ch", "ctx"),
            P("ch", "ctx"),
            P("ch"),
            P("ch", None),
            P("ch", None),
            P("ch", None),
            P("ch"),
        ),
        out_specs=(
            P("ch", "ctx"),
            P("ch"),
            P("ch", None),
            P("ch", None),
            P("ch", None),
            P("ch"),
            P("ctx"),
        ),
        check_vma=False,
    )
```

```python
import functools

import jax
import jax.numpy as jnp
from jax import lax
from jax.experimental import pallas as pl
from jax.experimental.pallas import tpu as pltpu
from jax.sharding import PartitionSpec as P

eps_norm = 1e-06
W = 128
GW = 16
PACK = W // GW
VMEM_LIMIT = 48 * 1024 * 1024


def passed_along(x, axis, by):
    count = lax.axis_size(axis)
    pairs = [(i, i + by) for i in range(count) if 0 <= i + by < count]
    return lax.ppermute(x, axis, pairs)


def exchanged(x, axis, bit):
    count = lax.axis_size(axis)
    return lax.ppermute(x, axis, [(i, i ^ bit) for i in range(count)])


def sum_over(x, axis):
    bit = 1
    while bit < lax.axis_size(axis):
        x = x + exchanged(x, axis, bit)
        bit *= 2
    return x


def states_after(total, rates, tokens):
    count = lax.axis_size("ctx")
    rank = lax.axis_index("ctx")
    into0 = jnp.zeros_like(rates)
    into1 = jnp.zeros_like(rates)
    bit = 1
    while bit < count:
        other = exchanged(total, "ctx", bit)
        o0, o1 = other[:, :GW], other[:, GW:]
        t0, t1 = total[:, :GW], total[:, GW:]
        lower = (rank & bit) == 0
        start = (rank // bit + 1) * bit
        gap = ((start - rank - 1) * tokens).astype(jnp.float32)
        factor = jnp.where(lower, jnp.exp(-rates * gap), 0.0)
        into0 = into0 + factor * o0
        into1 = into1 + factor * (o1 + gap * o0)
        if 2 * bit < count:
            span = float(bit * tokens)
            decay = jnp.exp(-rates * span)
            e0, e1 = jnp.where(lower, t0, o0), jnp.where(lower, t1, o1)
            l0, l1 = jnp.where(lower, o0, t0), jnp.where(lower, o1, t1)
            total = jnp.concatenate([e0 + decay * l0, e1 + decay * (l1 + span * l0)], axis=1)
        bit *= 2
    return jnp.concatenate([into0, into1], axis=1)


def dot(a, b, ca, cb):
    return lax.dot_general(
        a, b, (((ca,), (cb,)), ((), ())), preferred_element_type=jnp.float32
    )


def columns_of(row):
    return jnp.broadcast_to(row, (W, W)).T


def row_sums(stack):
    return jnp.sum(stack.T, axis=0, keepdims=True)


def split_two(x):
    high = x.astype(jnp.bfloat16)
    return high, (x - high.astype(jnp.float32)).astype(jnp.bfloat16)


def circulant(row):
    return pltpu.roll(jnp.broadcast_to(row, (W, W)), 0, 1, stride=1, stride_axis=0)


def diagonal_sums(x):
    half = W // 2
    while half >= 8:
        x = x[:half] + pltpu.roll(x[half:], W - half, 1)
        half //= 2
    for by in (4, 2, 1):
        x = x + pltpu.roll(pltpu.roll(x, W - by, 1), 8 - by, 0)
    return x[:1]


def tiles_of(ref, rows, blocks):
    return [ref[rows, W * k : W * (k + 1)] for k in range(blocks)]


def state_kernel(rate_ref, g_ref, ga_ref, s0_ref, s1_ref, total_ref, seg_rate_ref):
    blocks = g_ref.shape[1] // W
    rates = columns_of(rate_ref[0])
    lane_int = lax.broadcasted_iota(jnp.int32, (GW, W), 1)
    lane = lane_int.astype(jnp.float32)
    seg = lane_int // GW
    rate_seg = jnp.zeros((GW, W), jnp.float32)
    total0 = jnp.zeros((GW, W), jnp.float32)
    total1 = jnp.zeros((GW, W), jnp.float32)
    for q in range(PACK):
        rows = slice(GW * q, GW * (q + 1))
        r = rates[rows]
        fall = jnp.exp(-r * lane)
        table = jnp.concatenate(split_two(fall) + split_two(fall * lane), axis=0)
        data = jnp.concatenate(tiles_of(g_ref, rows, blocks)[1:] + [ga_ref[rows, :]], axis=0)
        sums = dot(table, data, 1, 1)
        s0 = sums[:GW] + sums[GW : 2 * GW]
        s1 = sums[2 * GW : 3 * GW] + sums[3 * GW :]
        by = 1
        while by < blocks:
            decay = jnp.exp(-r * float(W * by))
            keep = seg + by < blocks
            a0 = jnp.where(keep, pltpu.roll(s0, W - GW * by, 1), 0.0)
            a1 = jnp.where(keep, pltpu.roll(s1, W - GW * by, 1), 0.0)
            s1 = s1 + decay * (a1 + float(W * by) * a0)
            s0 = s0 + decay * a0
            by *= 2
        s0_ref[q] = s0
        s1_ref[q] = s1
        here = seg == q
        rate_seg = jnp.where(here, r, rate_seg)
        total0 = jnp.where(here, pltpu.roll(s0, GW * q, 1) if q else s0, total0)
        total1 = jnp.where(here, pltpu.roll(s1, GW * q, 1) if q else s1, total1)
    total_ref[0, :GW] = total0
    total_ref[0, GW:] = total1
    seg_rate_ref[0] = rate_seg


def main_kernel(
    rate_ref, res_ref, gain_ref, skip_ref, tap_ref, inv_ref, h_ref, hb_ref, g_ref, ga_ref,
    s0_ref, s1_ref, into_ref,
    ig_ref, tapg_ref, mom0_ref, mom1_ref, skipg_ref, gaing_ref, dot_ref,
):
    tokens = g_ref.shape[1]
    blocks = tokens // W
    rates = columns_of(rate_ref[0])
    residues = columns_of(res_ref[0])
    gains = columns_of(gain_ref[0])
    skips = columns_of(skip_ref[0])
    lane_int = lax.broadcasted_iota(jnp.int32, (GW, W), 1)
    lane = lane_int.astype(jnp.float32)
    seg = lane_int // GW
    upper = lax.broadcasted_iota(jnp.int32, (W, W), 1) >= lax.broadcasted_iota(
        jnp.int32, (W, W), 0
    )
    lower = lax.broadcasted_iota(jnp.int32, (W, W), 1) <= lax.broadcasted_iota(
        jnp.int32, (W, W), 0
    )
    back = jnp.where(lane_int == 0, 0.0, float(W) - lane)
    gap = float(W) - lane
    in0 = into_ref[0, :GW]
    in1 = into_ref[0, GW:]
    left = ((blocks - seg) * W).astype(jnp.float32)

    @pl.when(pl.program_id(0) == 0)
    def _():
        dot_ref[...] = jnp.zeros_like(dot_ref)

    inv_back = inv_ref[:, :W]
    inv = [inv_ref[:, W * (k + 1) : W * (k + 2)] for k in range(blocks)]
    moments0, moments1, skip_rows, gain_rows = [], [], [], []
    dots = None
    def one_group(q):
        rows = slice(GW * q, GW * (q + 1))
        r = rates[rows]
        amp = residues[rows] * jnp.sqrt(2.0 * r)
        gain = gains[rows]
        skip = skips[rows]
        to_end = jnp.exp(-r * gap)
        fall = jnp.where(lane_int == 0, 1.0, to_end)
        kern = jnp.sum(amp * fall, axis=0, keepdims=True)
        kern_two = jnp.concatenate(
            split_two(jnp.where(lower, circulant(kern), 0.0)), axis=0
        )
        circ = circulant(tap_ref[q : q + 1, :])
        now = jnp.where(upper, circ, 0.0).astype(jnp.bfloat16)
        before = jnp.where(upper, 0.0, circ).astype(jnp.bfloat16)
        normed = [t.astype(jnp.float32) * i for t, i in zip(tiles_of(h_ref, rows, blocks), inv)]
        units = [(n * gain).astype(jnp.bfloat16) for n in normed]
        unit_back = (hb_ref[rows, :].astype(jnp.float32) * inv_back * gain).astype(jnp.bfloat16)
        x_now = jnp.concatenate(units, axis=0)
        x_before = jnp.concatenate([unit_back] + units[:-1], axis=0)
        yield
        x_both = jnp.concatenate([x_now, x_before], axis=1)
        mixed = dot(x_both, jnp.concatenate([now, before], axis=0), 1, 0).astype(jnp.bfloat16)
        yield
        g_tiles = tiles_of(g_ref, rows, blocks)
        grads = jnp.concatenate(g_tiles, axis=0)
        grads_long = jnp.concatenate(g_tiles + [ga_ref[rows, :]], axis=0)
        a0in = jnp.where(seg == q, in0, 0.0)
        a1in = jnp.where(seg == q, in1, 0.0)
        for by in (GW, 2 * GW, 4 * GW):
            a0in = a0in + pltpu.roll(a0in, by, 1)
            a1in = a1in + pltpu.roll(a1in, by, 1)
        decay = jnp.exp(-r * left)
        after0 = s0_ref[q] + decay * a0in
        after1 = s1_ref[q] + decay * (a1in + left * a0in)
        yield
        a_high, a_low = split_two(jnp.concatenate([after0, a0in], axis=1))
        w_high, w_low = split_two(amp * to_end)
        outer = dot(
            jnp.concatenate([a_high, a_low, a_high], axis=0),
            jnp.concatenate([w_high, w_high, w_low], axis=0),
            0, 0,
        )[: W + GW]
        wide = grads_long.astype(jnp.float32)
        gm = (
            dot(jnp.concatenate([grads_long, grads_long], axis=1), kern_two, 1, 0)
            + outer
            + jnp.concatenate([skip] * (blocks + 1), axis=0) * wide
        ).astype(jnp.bfloat16)
        yield
        gm_now = gm[:W]
        ig = dot(
            jnp.concatenate([gm_now, gm[GW:]], axis=1),
            jnp.concatenate([now, before], axis=1),
            1, 1,
        )
        yield
        pairs = dot(gm_now, x_both, 0, 0)
        tapg_ref[q : q + 1, :] = diagonal_sums(jnp.where(lower, pairs[:, :W], pairs[:, W:]))
        lags = diagonal_sums(jnp.where(lower, dot(grads, mixed, 0, 0), 0.0))
        yield
        table = jnp.concatenate(split_two(to_end) + split_two(to_end * gap), axis=0)
        lifted = dot(table, mixed, 1, 1)
        l0 = lifted[:GW] + lifted[GW : 2 * GW]
        l1 = lifted[2 * GW : 3 * GW] + lifted[3 * GW :]
        yield
        near = lags * fall
        moments0.append(l0 * after0 + near)
        moments1.append(l1 * after0 + l0 * after1 + near * back)
        skip_terms = wide[:W] * mixed.astype(jnp.float32)
        gain_terms = ig * jnp.concatenate(normed, axis=0)
        skip_sum = skip_terms[:GW]
        gain_sum = gain_terms[:GW]
        for k in range(blocks):
            part = slice(GW * k, GW * (k + 1))
            ig_ref[rows, W * k : W * (k + 1)] = ig[part]
            if k:
                skip_sum = skip_sum + skip_terms[part]
                gain_sum = gain_sum + gain_terms[part]
        skip_rows.append(skip_sum)
        gain_rows.append(gain_sum)
        dot_ref[...] += gain_terms * jnp.concatenate([gain] * blocks, axis=0)
    for base in range(0, PACK, 4):
        running = [one_group(q) for q in range(base, base + 4)]
        while running:
            running = [group for group in running if next(group, True) is None]
    mom0_ref[0] = row_sums(jnp.concatenate(moments0, axis=0))
    mom1_ref[0] = row_sums(jnp.concatenate(moments1, axis=0))
    skipg_ref[0] = row_sums(jnp.concatenate(skip_rows, axis=0))
    gaing_ref[0] = row_sums(jnp.concatenate(gain_rows, axis=0))


def local(hidden, cotangent, norm_gain, mr_filter, residue, decay_rate, skip_weight):
    channels, tokens = hidden.shape
    groups = mr_filter.shape[0]
    ctx_count = lax.axis_size("ctx")
    full_width = channels * lax.axis_size("ch")
    grad_scale = (tokens * ctx_count) ** (-0.5)
    steps = groups // PACK
    f32 = jnp.float32

    hidden_back = passed_along(hidden[:, tokens - W :], "ctx", 1)
    cot_ahead = passed_along(cotangent[:, :W], "ctx", -1)

    def squares_of(x):
        wide = x.astype(f32)
        return jnp.sum(wide * wide, axis=0)

    squares = sum_over(jnp.concatenate([squares_of(hidden_back), squares_of(hidden)]), "ch")
    inverse_all = lax.rsqrt(squares / full_width + eps_norm)
    inverse_rms = inverse_all[W:]

    rate_rows = decay_rate.reshape(steps, 1, W)
    residue_rows = residue.reshape(steps, 1, W)
    gain_rows = norm_gain.reshape(steps, 1, W)
    skip_rows = skip_weight.reshape(steps, 1, W)

    row_spec = pl.BlockSpec((1, 1, W), lambda i: (i, 0, 0))
    wide_spec = pl.BlockSpec((W, tokens), lambda i: (i, 0))
    edge_spec = pl.BlockSpec((W, W), lambda i: (i, 0))
    state_spec = pl.BlockSpec((PACK, GW, W), lambda i: (i, 0, 0))
    row_shape = jax.ShapeDtypeStruct((steps, 1, W), f32)
    state_shape = jax.ShapeDtypeStruct((groups, GW, W), f32)

    state0, state1, total, seg_rates = pl.pallas_call(
        state_kernel,
        grid=(steps,),
        in_specs=[row_spec, wide_spec, edge_spec],
        out_specs=[
            state_spec, state_spec,
            pl.BlockSpec((1, 2 * GW, W), lambda i: (i, 0, 0)),
            pl.BlockSpec((1, GW, W), lambda i: (i, 0, 0)),
        ],
        out_shape=[
            state_shape, state_shape,
            jax.ShapeDtypeStruct((steps, 2 * GW, W), f32),
            jax.ShapeDtypeStruct((steps, GW, W), f32),
        ],
        compiler_params=pltpu.CompilerParams(vmem_limit_bytes=VMEM_LIMIT),
        cost_estimate=pl.CostEstimate(
            flops=groups * 2 * 64 * W * W, bytes_accessed=8 * 2**20, transcendentals=0
        ),
        name="states",
    )(rate_rows, cotangent, cot_ahead)
    into = states_after(total, seg_rates, tokens)

    input_grad, tap_part, mom0, mom1, skip_part, gain_part, dots = pl.pallas_call(
        main_kernel,
        grid=(steps,),
        in_specs=[
            row_spec, row_spec, row_spec, row_spec,
            pl.BlockSpec((PACK, W), lambda i: (i, 0)),
            pl.BlockSpec((1, tokens + W), lambda i: (0, 0)),
            wide_spec, edge_spec, wide_spec, edge_spec,
            state_spec, state_spec,
            pl.BlockSpec((1, 2 * GW, W), lambda i: (i, 0, 0)),
        ],
        out_specs=[
            wide_spec,
            pl.BlockSpec((PACK, W), lambda i: (i, 0)),
            row_spec, row_spec, row_spec, row_spec,
            pl.BlockSpec((W, W), lambda i: (0, 0)),
        ],
        out_shape=[
            jax.ShapeDtypeStruct((channels, tokens), f32),
            jax.ShapeDtypeStruct((groups, W), f32),
            row_shape, row_shape, row_shape, row_shape,
            jax.ShapeDtypeStruct((W, W), f32),
        ],
        compiler_params=pltpu.CompilerParams(vmem_limit_bytes=VMEM_LIMIT),
        cost_estimate=pl.CostEstimate(
            flops=groups * 24 * W**3, bytes_accessed=24 * 2**20, transcendentals=0
        ),
        name="main",
    )(
        rate_rows, residue_rows, gain_rows, skip_rows, mr_filter.astype(f32),
        inverse_all.reshape(1, tokens + W), hidden, hidden_back, cotangent, cot_ahead,
        state0, state1, into,
    )
    row_dot = sum_over(jnp.sum(dots.reshape(tokens // W, GW, W), axis=1).reshape(tokens), "ch")
    parts = jnp.concatenate(
        [tap_part] + [x.reshape(steps, W) for x in (mom0, mom1, skip_part, gain_part)], axis=0
    )
    whole = sum_over(parts, "ctx")
    tap_total = jnp.roll(whole[:groups, ::-1], 1, axis=1)
    first, second, skip_total, gain_total = (
        whole[groups + steps * i : groups + steps * (i + 1)] for i in range(4)
    )
    first_moment = first.reshape(decay_rate.shape)
    second_moment = second.reshape(decay_rate.shape)

    normed = hidden.astype(f32) * inverse_rms[None, :]
    pulled = input_grad * norm_gain[:, None]
    grad_inv_rms = row_dot / inverse_rms * full_width ** (-0.5)
    grad_hidden = (inverse_rms[None, :] * (pulled - normed * row_dot[None, :] / full_width)).astype(
        jnp.bfloat16
    )
    root_rate = jnp.sqrt(2.0 * decay_rate)
    grad_residue = root_rate * first_moment * grad_scale
    grad_log_rate = (
        residue * root_rate * (0.5 * first_moment - decay_rate * second_moment) * grad_scale
    )
    return (
        grad_hidden,
        gain_total.reshape(channels) * grad_scale,
        tap_total * grad_scale,
        grad_residue,
        grad_log_rate,
        skip_total.reshape(channels) * grad_scale,
        grad_inv_rms,
    )


def solution(mesh):
    return jax.shard_map(
        local,
        mesh=mesh,
        in_specs=(
            P("ch", "ctx"),
            P("ch", "ctx"),
            P("ch"),
            P("ch", None),
            P("ch", None),
            P("ch", None),
            P("ch"),
        ),
        out_specs=(
            P("ch", "ctx"),
            P("ch"),
            P("ch", None),
            P("ch", None),
            P("ch", None),
            P("ch"),
            P("ctx"),
        ),
        check_vma=False,
    )
```
